512 devices in a mesh: space: 32 (over z_lo, y, core), chan: 4 (over z_hi), batch: 4 (over x).
Axes of the slice: x: 4, y: 4, z: 16 (z_hi: 4, z_lo: 4; z = z_hi * 4 + z_lo), core: 2. Of those that a mesh axis runs over, the one named last changes fastest.
Arguments:
- crops: bfloat16 [4, 32, 64, 48, 128], P('batch', 'chan', 'space'), may hold values from -6 to 6
- cotangent: bfloat16 [4, 32, 64, 48, 128], P('batch', 'chan', 'space'), may hold values from -6 to 6
- weights: bfloat16 [32, 27, 32], replicated, may hold values from -0.21875 to 0.21875
Outputs:
- activated: bfloat16 [4, 32, 64, 48, 128], P('batch', 'chan', 'space')
- input_grad: bfloat16 [4, 32, 64, 48, 128], P('batch', 'chan', 'space')
- weight_grad: float32 [32, 27, 32], replicated
The draws below stay inside these ranges and needn't reach their ends.
All inputs are finite; a program needn't handle non-finite values.
Results may differ from the reference program's by a relative error of at most 0.013.
Values may be sent and summed in bfloat16 or wider, within the bound.
No kernel may reach another device: no remote copies, remote signals or barrier semaphores. Data moves between devices by JAX's collectives and lax.ppermute only.
A program may use at most 64 MiB of HBM per device.

```python
import jax
import jax.numpy as jnp
from jax import lax

C = 32
CY = 48
CZ = 128
NX = 64
BATCH = 4
N_CHAN = 4


def shard_levels(stream_key, extent, cuts, least, high):
    factor_of = 1.0
    for dim, shards_of in cuts:
        heights = jax.random.uniform(jax.random.fold_in(jax.random.fold_in(stream_key, 6), dim), (shards_of,), jnp.float32, least / len(cuts), high / len(cuts))
        factor_of = factor_of * jnp.repeat(jnp.exp(heights), extent[dim] // shards_of).reshape((-1,) + (1,) * (len(extent) - 1 - dim))
    return factor_of


def noise(own_key, dims, scale, most, pieces=(), kind=jnp.bfloat16):
    drawn = scale * jax.random.normal(own_key, dims, jnp.float32)
    if pieces:
        drawn = drawn * shard_levels(own_key, dims, pieces, -0.22, 0.18)
    return jnp.clip(drawn, -most, most).astype(kind)


def setup_inputs(seed: int = 0) -> dict:
    seeds = jax.random.split(jax.random.key(seed), 4)
    crops = noise(seeds[0], (BATCH, C, NX, CY, CZ), 1.0, 6.0, ((0, 4), (1, 4), (2, 32)))
    cotangent = noise(seeds[1], (BATCH, C, NX, CY, CZ), 1.0, 6.0, ((0, 4), (1, 4), (2, 32)))
    weights = noise(seeds[2], (C, 27, C), (27 * C) ** -0.5, 0.21875)
    return {"crops": crops, "cotangent": cotangent, "weights": weights}


def group_conv(field, kernel):
    outs = kernel.shape[0]
    ins = kernel.shape[2]
    rhs = jnp.transpose(kernel.reshape(outs, 3, 3, 3, ins), (0, 4, 1, 2, 3))
    result = lax.conv_general_dilated(field[None], rhs, (1, 1, 1), ((1, 1), (1, 1), (1, 1)), dimension_numbers=('NCDHW', 'OIDHW', 'NCDHW'), preferred_element_type=jnp.float32)
    return result[0]

def rounded(value):
    return lax.optimization_barrier(value.astype(jnp.bfloat16)).astype(jnp.float32)

def reference(crops, cotangent, weights):
    share = C // N_CHAN
    flipped = jnp.transpose(weights[:, ::-1, :], (2, 1, 0))

    def one_crop(pair):
        field, upper = pair
        pre = jnp.zeros((C, NX, CY, CZ), jnp.float32)
        for group in range(N_CHAN):
            low = group * share
            pre = pre + rounded(group_conv(field[low:low + share], weights[:, :, low:low + share]))
        below = jnp.minimum(pre, 0.0)
        activated = jnp.where(pre > 0, pre, jnp.expm1(below)).astype(jnp.bfloat16)
        wide_upper = upper.astype(jnp.float32)
        upstream = jnp.where(pre > 0, wide_upper, wide_upper * jnp.exp(below)).astype(jnp.bfloat16)
        back = jnp.zeros((C, NX, CY, CZ), jnp.float32)
        for group in range(N_CHAN):
            low = group * share
            back = back + rounded(group_conv(upstream[low:low + share], flipped[:, :, low:low + share]))
        padded = jnp.pad(field, ((0, 0), (1, 1), (1, 1), (1, 1)))
        wide_up = upstream.astype(jnp.float32)
        columns = []
        for tap_a in range(3):
            for tap_b in range(3):
                for tap_c in range(3):
                    shifted = padded[:, tap_a:tap_a + NX, tap_b:tap_b + CY, tap_c:tap_c + CZ].astype(jnp.float32)
                    columns.append(jnp.einsum('oxyz,ixyz->oi', wide_up, shifted, precision=lax.Precision.HIGHEST))
        return (activated, back.astype(jnp.bfloat16), jnp.stack(columns, 1))
    activated, input_grad, partial_grads = lax.map(one_crop, (crops, cotangent))
    weight_grad = lax.optimization_barrier(jnp.sum(partial_grads, axis=0)) / jnp.sqrt(jnp.float32(BATCH * NX * CY * CZ))
    return (activated, input_grad, weight_grad)
```

```python
import functools

import jax
import jax.numpy as jnp
from jax import lax
from jax.experimental import pallas as pl
from jax.experimental.pallas import tpu as pltpu
from jax.sharding import PartitionSpec as P

LANES = 128
F32 = jnp.float32
BF16 = jnp.bfloat16


def iota(shape, dim):
    return lax.broadcasted_iota(jnp.int32, shape, dim)


def one_hot(hit):
    return jnp.where(hit, 1.0, 0.0)


def dot(left, right, **options):
    return jnp.dot(left, right, preferred_element_type=F32, **options)


def shifted(block, step):
    moved = pltpu.roll(block, step % LANES, 1)
    lane = iota(block.shape, 1)
    edge = 0 if step == 1 else LANES - 1
    return jnp.where(lane == edge, 0.0, moved)


def pack_kernel(crops, cotangent, out):
    both = jnp.concatenate([crops[...].reshape(768, LANES), cotangent[...].reshape(768, LANES)], axis=1)
    for part in range(4):
        row = iota((256, 768), 0)
        y = row // 16 + (12 * part - 2)
        source = (row % 8) * 96 + (row // 8 % 2) * 48 + y
        source = jnp.where((y >= 0) & (y < 48), source, -1)
        move = one_hot(source == iota((256, 768), 1)).astype(BF16)
        moved = dot(move, both).astype(BF16).reshape(16, 16, 2 * LANES)
        out[part, 0:16] = moved[:, :, :LANES]
        out[part, 16:30] = moved[1:15, :, LANES:]


def unpack_kernel(back, activated, input_grad):
    rows = [back[:, which].reshape(768, LANES) for which in range(2)]
    both = jnp.concatenate(rows, axis=1)
    row = iota((768, 768), 0)
    source = (row % 48) * 16 + (row // 48 % 2) * 8 + row // 96
    move = one_hot(source == iota((768, 768), 1)).astype(BF16)
    moved = dot(move, both).astype(BF16)
    activated[...] = moved[:, :LANES].reshape(8, 2, 48, LANES)
    input_grad[...] = moved[:, LANES:].reshape(8, 2, 48, LANES)


def main_kernel(before, own, after, by_out, by_in, back, grads, field, forward, backward, upper, sides):
    slabs = (before, own, after)
    for row in range(16):
        for slab in range(3):
            field[slab * 64 : slab * 64 + 64, row * LANES : (row + 1) * LANES] = slabs[slab][:, row].reshape(64, LANES)

    column = iota((32, 192), 1)
    spread = one_hot(column // 16 % 4 * 8 + column % 8 == iota((32, 192), 0)).astype(BF16)
    wide = dot(by_out[...], spread)
    column = iota((8, 192), 1)
    plane = column // 64 * 2 + column // 8 % 2
    for c in range(3):
        for b in range(3):

            def band(group, target):
                total = jnp.zeros((8, 192), F32)
                for a in range(3):
                    low = (9 * a + 3 * b + c) * 32 + group * 8
                    total = jnp.where(plane == target + a - 1, wide[low : low + 8], total)
                return total

            pieces = [band(group, 2 + x) for group in range(4) for x in range(2)]
            pieces += [band(group, 1) for group in range(4)]
            pieces += [band(group, 4) for group in range(4)]
            forward[b, c * 128 : c * 128 + 128] = jnp.concatenate(pieces, axis=0).astype(BF16)

    column = iota((32, 128), 1)
    channel = jnp.where(column < 64, column // 16 * 8 + column % 8, column % 32)
    wide_in = dot(by_in[...], one_hot(channel == iota((32, 128), 0)).astype(BF16))
    column = iota((8, 128), 1)
    plane_in = jnp.where(column < 64, 2 + column // 8 % 2, jnp.where(column < 96, 1, 4))
    for c in range(3):
        for b in range(3):
            pieces = []
            for group in range(4):
                for x in range(2):
                    total = jnp.zeros((8, 128), F32)
                    for a in range(3):
                        low = (26 - (9 * a + 3 * b + c)) * 32 + group * 8
                        total = jnp.where(plane_in == 1 + x + a, wide_in[low : low + 8], total)
                    pieces.append(total)
            backward[b, c * 64 : c * 64 + 64] = jnp.concatenate(pieces, axis=0).astype(BF16)

    for pair in range(7):
        low = pair * 2
        total = sum(dot(forward[b], field[:, (low + b) * LANES : (low + b + 2) * LANES]) for b in range(3))
        for side in range(2):
            row = low + side
            cut = total[:, side * LANES : (side + 1) * LANES]
            pre = cut[128:256] + shifted(cut[0:128], 1) + shifted(cut[256:384], -1)
            power = jnp.exp(jnp.minimum(pre, 0.0))
            if 1 <= row <= 12:
                activated = jnp.where(pre[:64] > 0, pre[:64], power[:64] - 1.0).astype(BF16)
                back[:, 0, row - 1] = activated.reshape(4, 16, LANES)
            cot_own = own[:, 16 + row].astype(F32).reshape(64, LANES)
            cot_before = before[:, 16 + row].astype(F32)[:, 8:16].reshape(32, LANES)
            cot_after = after[:, 16 + row].astype(F32)[:, 0:8].reshape(32, LANES)
            cot = jnp.concatenate([cot_own, cot_before, cot_after], axis=0)
            up = jnp.where(pre > 0, cot, cot * power).astype(BF16)
            upper[:, row * LANES : (row + 1) * LANES] = up
            if 1 <= row <= 12:
                here = slice((row - 1) * LANES, row * LANES)
                wide_up = up[:64].astype(F32)
                sides[0:64, here] = shifted(wide_up, -1).astype(BF16)
                sides[64:128, here] = up[:64]
                sides[128:192, here] = shifted(wide_up, 1).astype(BF16)

    for pair in range(6):
        low = pair * 2
        total = sum(dot(backward[b], upper[:, (low + b) * LANES : (low + b + 2) * LANES]) for b in range(3))
        for side in range(2):
            cut = total[:, side * LANES : (side + 1) * LANES]
            grad = cut[64:128] + shifted(cut[0:64], 1) + shifted(cut[128:192], -1)
            back[:, 1, low + side] = grad.astype(BF16).reshape(4, 16, LANES)

    row = iota((192, 256), 0)
    col = iota((192, 256), 1)
    row_plane = row // 64 * 2 + row // 8 % 2
    same = row // 16 % 4 * 8 + row % 8 == col % 32
    row9 = iota((192, 128), 0)
    col9 = iota((192, 128), 1)
    plane9 = row9 // 64 * 2 + row9 // 8 % 2
    same9 = row9 // 16 % 4 * 8 + row9 % 8 == col9 % 32
    eight = jnp.zeros((96, 256), F32)
    ninth = jnp.zeros((32, 128), F32)
    for b in range(3):
        product = lax.dot_general(
            sides[...],
            field[:, (1 + b) * LANES : (13 + b) * LANES],
            (((1,), (1,)), ((), ())),
            preferred_element_type=F32,
        ).reshape(12, 2, 8, 192)
        for x in range(2):
            part = product[:, x].reshape(96, 192)
            pick = same & (col // 32 % 3 == b) & (row_plane == 1 + x + col // 96)
            eight = eight + dot(part, one_hot(pick), precision=lax.Precision.HIGHEST)
            if b == 2:
                for c in range(3):
                    pick = same9 & (col9 // 32 == c) & (plane9 == 3 + x)
                    ninth = ninth + dot(part[c * 32 : c * 32 + 32], one_hot(pick), precision=lax.Precision.HIGHEST)
    for c in range(3):
        for half in range(2):
            cut = eight[c * 32 : c * 32 + 32, half * LANES : (half + 1) * LANES]
            grads[(c * 2 + half) * 4 : (c * 2 + half) * 4 + 4] = cut.reshape(4, 8, LANES)
    grads[24:28] = ninth.reshape(4, 8, LANES)
    grads[28:32] = jnp.zeros((4, 8, LANES), F32)


def call(kernel, outs, scratch=(), flops=0, moved=0):
    vmem = pl.BlockSpec(memory_space=pltpu.VMEM)
    return pl.pallas_call(
        kernel,
        out_shape=outs,
        out_specs=jax.tree.map(lambda _: vmem, outs),
        scratch_shapes=scratch,
        compiler_params=pltpu.CompilerParams(vmem_limit_bytes=48 * 1024 * 1024),
        cost_estimate=pl.CostEstimate(flops=flops, bytes_accessed=moved, transcendentals=0),
    )


def body(crops, cotangent, weights):
    space = lax.axis_size("space")
    outer = lax.axis_size("chan") * lax.axis_size("batch")
    up = [(i, i + 1) for i in range(space - 1)]
    down = [(i + 1, i) for i in range(space - 1)]
    packed = call(pack_kernel, jax.ShapeDtypeStruct((4, 30, 16, LANES), BF16))(crops[0], cotangent[0])
    own = lax.all_to_all(packed, "chan", 0, 0)
    before = lax.ppermute(own, "space", up)
    after = lax.ppermute(own, "space", down)
    by_out = jnp.transpose(weights, (1, 0, 2)).reshape(864, 32)
    by_in = jnp.transpose(weights, (1, 2, 0)).reshape(864, 32)
    back, grads = call(
        main_kernel,
        (
            jax.ShapeDtypeStruct((4, 2, 12, 16, LANES), BF16),
            jax.ShapeDtypeStruct((32, 8, LANES), F32),
        ),
        [
            pltpu.VMEM((192, 16 * LANES), BF16),
            pltpu.VMEM((3, 384, 192), BF16),
            pltpu.VMEM((3, 192, 128), BF16),
            pltpu.VMEM((128, 14 * LANES), BF16),
            pltpu.VMEM((192, 12 * LANES), BF16),
        ],
    )(before, own, after, by_out, by_in)
    slab = jax.ShapeDtypeStruct((8, 2, 48, LANES), BF16)
    activated, input_grad = call(unpack_kernel, (slab, slab))(lax.all_to_all(back, "chan", 0, 0))

    tiles = 32 // space
    terms = lax.all_to_all(grads.reshape(space, tiles, 8, LANES), "space", 0, 0)
    share = jnp.sum(terms, axis=0)
    terms = lax.all_to_all(jnp.broadcast_to(share, (outer,) + share.shape), ("chan", "batch"), 0, 0)
    cells = lax.axis_size("batch") * space * crops.shape[2] * crops.shape[3] * crops.shape[4]
    share = jnp.sum(terms, axis=0) / jnp.sqrt(jnp.float32(cells))
    whole = lax.all_to_all(jnp.broadcast_to(share, (space,) + share.shape), "space", 0, 0).reshape(32, 8, LANES)
    eight = whole[:24].reshape(3, 2, 4, 8, 4, 32).transpose(2, 3, 1, 4, 0, 5).reshape(32, 8, 3, 32)
    ninth = whole[24:28].reshape(32, 1, 4, 32)[:, :, :3]
    weight_grad = jnp.concatenate([eight, ninth], axis=1).reshape(32, 27, 32)
    return activated[None], input_grad[None], weight_grad


def solution(mesh):
    return jax.shard_map(
        body,
        mesh=mesh,
        in_specs=(
            P("batch", "chan", "space", None, None),
            P("batch", "chan", "space", None, None),
            P(),
        ),
        out_specs=(
            P("batch", "chan", "space", None, None),
            P("batch", "chan", "space", None, None),
            P(),
        ),
        check_vma=False,
    )
```

```python
import functools

import jax
import jax.numpy as jnp
from jax import lax
from jax.experimental import pallas as pl
from jax.experimental.pallas import tpu as pltpu
from jax.sharding import Mesh, PartitionSpec as P

LANES = 128
F32 = jnp.float32
BF16 = jnp.bfloat16


def iota(shape, dim):
    return lax.broadcasted_iota(jnp.int32, shape, dim)


def one_hot(hit):
    return jnp.where(hit, 1.0, 0.0)


def dot(left, right, **options):
    return jnp.dot(left, right, preferred_element_type=F32, **options)


def split(block):
    high = block.astype(BF16)
    rest = block - high.astype(F32)
    middle = rest.astype(BF16)
    low = (rest - middle.astype(F32)).astype(BF16)
    return jnp.concatenate([high, middle, low], axis=0)


def shifted(block, step):
    moved = pltpu.roll(block, step % LANES, 1)
    lane = iota(block.shape, 1)
    edge = 0 if step == 1 else LANES - 1
    return jnp.where(lane == edge, 0.0, moved)


def pack_kernel(place, crops, cotangent, *outs):
    row = iota((256, LANES), 0)
    lane = iota((256, LANES), 1)
    base = (row & 7) * 96 + (row >> 3 & 1) * 48
    moves = []
    for step in range(4):
        part = (place[0] + step) & 3
        y = (row >> 4) + (12 * part - 2)
        source = jnp.where((y >= 0) & (y < 48), base + y, -1)
        tiles = [one_hot(source == lane + k * LANES).astype(BF16) for k in range(6)]
        moves.append(jnp.concatenate(tiles, axis=1))
    both = jnp.concatenate([crops[...].reshape(768, LANES), cotangent[...].reshape(768, LANES)], axis=1)
    for move, out in zip(moves, outs):
        moved = dot(move, both).astype(BF16).reshape(16, 16, 2 * LANES)
        out[0:16] = moved[:, :, :LANES]
        out[16:30] = moved[1:15, :, LANES:]


def unpack_kernel(place, *refs):
    parts, (activated, input_grad) = refs[:4], refs[4:]
    rows = [
        jnp.concatenate([part[which * 12 : which * 12 + 12].reshape(192, LANES) for part in parts], axis=0)
        for which in range(2)
    ]
    both = jnp.concatenate(rows, axis=1)
    outer = iota((16, 48, LANES), 0)
    y = iota((16, 48, LANES), 1)
    part = (y >= 12).astype(jnp.int32) + (y >= 24).astype(jnp.int32) + (y >= 36).astype(jnp.int32)
    step = (part + 4 - place[0]) & 3
    source = (step * 192 + (y - 12 * part) * 16 + (outer & 1) * 8 + (outer >> 1)).reshape(768, LANES)
    lane = iota((768, LANES), 1)
    move = jnp.concatenate([one_hot(source == lane + k * LANES).astype(BF16) for k in range(6)], axis=1)
    moved = dot(move, both).astype(BF16)
    activated[...] = moved[:, :LANES].reshape(8, 2, 48, LANES)
    input_grad[...] = moved[:, LANES:].reshape(8, 2, 48, LANES)


def band_kernel(by_out, by_in, forward, backward):
    column = iota((32, 192), 1)
    spread = one_hot(column // 16 % 4 * 8 + column % 8 == iota((32, 192), 0)).astype(BF16)
    wide = dot(by_out[...], spread)
    column = iota((8, 192), 1)
    plane = column // 64 * 2 + column // 8 % 2
    for c in range(3):
        for b in range(3):

            def band(group, target):
                total = jnp.zeros((8, 192), F32)
                for a in range(3):
                    low = (9 * a + 3 * b + c) * 32 + group * 8
                    total = jnp.where(plane == target + a - 1, wide[low : low + 8], total)
                return total

            pieces = [band(group, 2 + x) for group in range(4) for x in range(2)]
            pieces += [band(group, 1) for group in range(4)]
            pieces += [band(group, 4) for group in range(4)]
            forward[b, c * 128 : c * 128 + 128] = jnp.concatenate(pieces, axis=0).astype(BF16)

    column = iota((32, 128), 1)
    channel = jnp.where(column < 64, column // 16 * 8 + column % 8, column % 32)
    wide_in = dot(by_in[...], one_hot(channel == iota((32, 128), 0)).astype(BF16))
    column = iota((8, 128), 1)
    plane_in = jnp.where(column < 64, 2 + column // 8 % 2, jnp.where(column < 96, 1, 4))
    for c in range(3):
        for b in range(3):
            pieces = []
            for group in range(4):
                for x in range(2):
                    total = jnp.zeros((8, 128), F32)
                    for a in range(3):
                        low = (26 - (9 * a + 3 * b + c)) * 32 + group * 8
                        total = jnp.where(plane_in == 1 + x + a, wide_in[low : low + 8], total)
                    pieces.append(total)
            backward[b, c * 64 : c * 64 + 64] = jnp.concatenate(pieces, axis=0).astype(BF16)


def forward_kernel(place, *refs):
    parts, refs = refs[:9], refs[9:]
    forward, activated, upper, grads, field, cots, sides = refs
    member, core = place[0], place[1]

    for s in range(4):
        group = (member + s) & 3
        mine, near, far = parts[(0, 6, 3, 3)[s] :][:3]
        base = 30 if s == 3 else 0
        near_row = pl.multiple_of((1 - core) * 128 + group * 16, 16)
        far_row = pl.multiple_of(core * 128 + group * 16, 16)
        own_row = pl.multiple_of(64 + group * 16, 16)
        for row in range(16):
            here = slice(row * LANES, (row + 1) * LANES)
            field[pl.ds(near_row, 16), here] = near[base + row]
            field[pl.ds(own_row, 16), here] = mine[base + row]
            field[pl.ds(far_row, 16), here] = far[base + row]
        cot_row = pl.multiple_of(group * 16, 16)
        near_cot = pl.multiple_of(64 + (1 - core) * 32 + group * 8, 8)
        far_cot = pl.multiple_of(64 + core * 32 + group * 8, 8)
        for row in range(14):
            here = slice(row * LANES, (row + 1) * LANES)
            cots[pl.ds(cot_row, 16), here] = mine[base + 16 + row].astype(F32)
            wide_near = near[base + 16 + row].astype(F32)
            wide_far = far[base + 16 + row].astype(F32)
            cots[pl.ds(near_cot, 8), here] = jnp.where(core == 0, wide_near[0:8], wide_near[8:16])
            cots[pl.ds(far_cot, 8), here] = jnp.where(core == 0, wide_far[8:16], wide_far[0:8])

    for pair in range(7):
        low = pair * 2
        total = sum(dot(forward[b], field[:, (low + b) * LANES : (low + b + 2) * LANES]) for b in range(3))
        for side in range(2):
            row = low + side
            cut = total[:, side * LANES : (side + 1) * LANES]
            pre = cut[128:256] + shifted(cut[0:128], 1) + shifted(cut[256:384], -1)
            power = jnp.exp(jnp.minimum(pre, 0.0))
            if 1 <= row <= 12:
                result = jnp.where(pre[:64] > 0, pre[:64], power[:64] - 1.0).astype(BF16)
                activated[:, (row - 1) * LANES : row * LANES] = result
            cot = cots[:, row * LANES : (row + 1) * LANES]
            up = jnp.where(pre > 0, cot, cot * power).astype(BF16)
            upper[:, row * LANES : (row + 1) * LANES] = up
            if 1 <= row <= 12:
                here = slice((row - 1) * LANES, row * LANES)
                wide_up = up[:64].astype(F32)
                sides[0:64, here] = shifted(wide_up, -1).astype(BF16)
                sides[64:128, here] = up[:64]
                sides[128:192, here] = shifted(wide_up, 1).astype(BF16)

    row = iota((192, 256), 0)
    col = iota((192, 256), 1)
    row_plane = row // 64 * 2 + row // 8 % 2
    same = row // 16 % 4 * 8 + row % 8 == col % 32
    row9 = iota((192, 128), 0)
    col9 = iota((192, 128), 1)
    plane9 = row9 // 64 * 2 + row9 // 8 % 2
    same9 = row9 // 16 % 4 * 8 + row9 % 8 == col9 % 32
    eight = jnp.zeros((96, 256), F32)
    ninth = jnp.zeros((32, 128), F32)
    for b in range(3):
        product = lax.dot_general(
            sides[...],
            field[:, (1 + b) * LANES : (13 + b) * LANES],
            (((1,), (1,)), ((), ())),
            preferred_element_type=F32,
        ).reshape(12, 2, 8, 192)
        for x in range(2):
            part = split(product[:, x].reshape(96, 192))
            pick = same & (col // 32 % 3 == b) & (row_plane == 1 + x + col // 96)
            picked = dot(part, one_hot(pick).astype(BF16))
            eight = eight + (picked[0:96] + picked[96:192] + picked[192:288])
            if b == 2:
                for c in range(3):
                    pick = same9 & (col9 // 32 == c) & (plane9 == 3 + x)
                    rows = [part[k * 96 + c * 32 : k * 96 + c * 32 + 32] for k in range(3)]
                    picked = dot(jnp.concatenate(rows, axis=0), one_hot(pick).astype(BF16))
                    ninth = ninth + (picked[0:32] + picked[32:64] + picked[64:96])
    for c in range(3):
        for half in range(2):
            cut = eight[c * 32 : c * 32 + 32, half * LANES : (half + 1) * LANES]
            grads[(c * 2 + half) * 4 : (c * 2 + half) * 4 + 4] = cut.reshape(4, 8, LANES)
    grads[24:28] = ninth.reshape(4, 8, LANES)
    grads[28:32] = jnp.zeros((4, 8, LANES), F32)


def backward_kernel(place, activated, upper, backward, *refs):
    backs, results = refs[:4], refs[4]
    member = place[0]
    for pair in range(6):
        low = pair * 2
        total = sum(dot(backward[b], upper[:, (low + b) * LANES : (low + b + 2) * LANES]) for b in range(3))
        for side in range(2):
            cut = total[:, side * LANES : (side + 1) * LANES]
            grad = cut[64:128] + shifted(cut[0:64], 1) + shifted(cut[128:192], -1)
            results[:, (low + side) * LANES : (low + side + 1) * LANES] = grad.astype(BF16)

    for step, back in enumerate(backs):
        for which, source in enumerate((activated, results)):
            low = pl.multiple_of(((member + step) & 3) * 16, 16)
            for row in range(12):
                back[which * 12 + row] = source[pl.ds(low, 16), row * LANES : (row + 1) * LANES]


def call(kernel, outs, scratch=(), place=False, flops=0, moved=0):
    vmem = pl.BlockSpec(memory_space=pltpu.VMEM)
    smem = pl.BlockSpec(memory_space=pltpu.SMEM)

    def run(*args):
        specs = [vmem] * len(args)
        if place:
            specs[0] = smem
        return pl.pallas_call(
            kernel,
            out_shape=outs,
            in_specs=specs,
            out_specs=jax.tree.map(lambda _: vmem, outs),
            scratch_shapes=scratch,
            compiler_params=pltpu.CompilerParams(vmem_limit_bytes=48 * 1024 * 1024),
            cost_estimate=pl.CostEstimate(flops=flops, bytes_accessed=moved, transcendentals=0),
        )(*args)

    return run


def reshard(parts):
    got = [parts[0], None, None, None]
    for step in (2, 1, 3):
        got[4 - step] = lax.ppermute(parts[step], "chan", [(i, (i + step) % 4) for i in range(4)])
    return got


def body(crops, cotangent, weights):
    place = jnp.stack([lax.axis_index("chan"), lax.axis_index("core")]).astype(jnp.int32)
    piece = jax.ShapeDtypeStruct((30, 16, LANES), BF16)
    packed = call(pack_kernel, (piece,) * 4, place=True, flops=10**9)(place, crops[0], cotangent[0])
    got = reshard(packed)
    chips = lax.axis_size("zlo") * lax.axis_size("y")
    remote = [(2 * i + 1, 2 * i + 2) for i in range(chips - 1)]
    remote += [(j, i) for i, j in remote]
    parts = []
    for mine in (got[0], jnp.concatenate([got[2], got[3]], axis=0), got[1]):
        near = lax.ppermute(mine, "core", [(0, 1), (1, 0)])
        far = lax.ppermute(mine, ("zlo", "y", "core"), remote)
        parts += [mine, near, far]
    by_out = jnp.transpose(weights, (1, 0, 2)).reshape(864, 32)
    by_in = jnp.transpose(weights, (1, 2, 0)).reshape(864, 32)
    forward, backward = call(
        band_kernel,
        (jax.ShapeDtypeStruct((3, 384, 192), BF16), jax.ShapeDtypeStruct((3, 192, 128), BF16)),
        flops=10**9,
    )(by_out, by_in)
    rows = jax.ShapeDtypeStruct((64, 12 * LANES), BF16)
    activated, upper, grads = call(
        forward_kernel,
        (rows, jax.ShapeDtypeStruct((128, 14 * LANES), BF16), jax.ShapeDtypeStruct((32, 8, LANES), F32)),
        [
            pltpu.VMEM((192, 16 * LANES), BF16),
            pltpu.VMEM((128, 14 * LANES), F32),
            pltpu.VMEM((192, 12 * LANES), BF16),
        ],
        place=True,
        flops=3 * 10**9,
    )(place, *parts, forward)
    piece = jax.ShapeDtypeStruct((24, 16, LANES), BF16)
    backs = call(
        backward_kernel,
        (piece,) * 4,
        [pltpu.VMEM((64, 12 * LANES), BF16)],
        place=True,
        flops=2 * 10**9,
    )(place, activated, upper, backward)
    slab = jax.ShapeDtypeStruct((8, 2, 48, LANES), BF16)
    activated, input_grad = call(unpack_kernel, (slab, slab), place=True, flops=10**9)(place, *reshard(backs))

    plane = ("y", "core", "batch")
    column = ("zlo", "chan")
    pieces, rest = lax.axis_size(plane), lax.axis_size(column)
    terms = lax.all_to_all(grads.reshape((pieces, -1) + grads.shape[1:]), plane, 0, 0)
    share = jnp.sum(terms, axis=0)
    terms = lax.all_to_all(jnp.broadcast_to(share, (rest,) + share.shape), column, 0, 0)
    cells = pieces * rest // lax.axis_size("chan") * crops.shape[2] * crops.shape[3] * crops.shape[4]
    share = jnp.sum(terms, axis=0) / jnp.sqrt(jnp.float32(cells))
    whole = lax.all_to_all(jnp.broadcast_to(share, (pieces,) + share.shape), plane, 0, 0).reshape(32, 8, LANES)
    eight = whole[:24].reshape(3, 2, 4, 8, 4, 32).transpose(2, 3, 1, 4, 0, 5).reshape(32, 8, 3, 32)
    ninth = whole[24:28].reshape(32, 1, 4, 32)[:, :, :3]
    weight_grad = jnp.concatenate([eight, ninth], axis=1).reshape(32, 27, 32)
    return activated[None], input_grad[None], weight_grad


def solution(mesh):
    space, chan, batch = (mesh.shape[name] for name in ("space", "chan", "batch"))
    cut = mesh.devices.reshape(space // 8, 4, 2, chan, batch)
    fine = Mesh(cut, ("zlo", "y", "core", "chan", "batch"))
    spec = P("batch", "chan", ("zlo", "y", "core"), None, None)
    return jax.shard_map(
        body,
        mesh=fine,
        in_specs=(spec, spec, P()),
        out_specs=(spec, spec, P()),
        check_vma=False,
    )
```

```python
import functools

import jax
import jax.numpy as jnp
from jax import lax
from jax.experimental import pallas as pl
from jax.experimental.pallas import tpu as pltpu
from jax.sharding import Mesh, PartitionSpec as P

LANES = 128
F32 = jnp.float32
BF16 = jnp.bfloat16


def iota(shape, dim):
    return lax.broadcasted_iota(jnp.int32, shape, dim)


def one_hot(hit):
    return jnp.where(hit, 1.0, 0.0)


def dot(left, right, **options):
    return jnp.dot(left, right, preferred_element_type=F32, **options)


def split(block):
    high = block.astype(BF16)
    rest = block - high.astype(F32)
    middle = rest.astype(BF16)
    low = (rest - middle.astype(F32)).astype(BF16)
    return jnp.concatenate([high, middle, low], axis=0)


def shifted(block, step):
    moved = pltpu.roll(block, step % LANES, 1)
    lane = iota(block.shape, 1)
    edge = 0 if step == 1 else LANES - 1
    return jnp.where(lane == edge, 0.0, moved)


def pack_kernel(place, crops, cotangent, *outs):
    row = iota((256, LANES), 0)
    lane = iota((256, LANES), 1)
    base = (row & 7) * 96 + (row >> 3 & 1) * 48
    moves = []
    for step in range(4):
        part = (place[0] + step) & 3
        y = (row >> 4) + (12 * part - 2)
        source = jnp.where((y >= 0) & (y < 48), base + y, -1)
        tiles = [one_hot(source == lane + k * LANES).astype(BF16) for k in range(6)]
        moves.append(jnp.concatenate(tiles, axis=1))
    both = jnp.concatenate([crops[...].reshape(768, LANES), cotangent[...].reshape(768, LANES)], axis=1)
    for move, out in zip(moves, outs):
        moved = dot(move, both).astype(BF16).reshape(16, 16, 2 * LANES)
        out[0:14] = moved[1:15, :, :LANES]
        out[14:26] = moved[2:14, :, LANES:]


def unpack_kernel(place, *refs):
    parts, (activated, input_grad) = refs[:4], refs[4:]
    outer = iota((16, 48, LANES), 0)
    y = iota((16, 48, LANES), 1)
    part = (y >= 12).astype(jnp.int32) + (y >= 24).astype(jnp.int32) + (y >= 36).astype(jnp.int32)
    row = y - 12 * part
    inner = (outer & 1) * 8 + (outer >> 1)
    step = (part + 4 - place[0]) & 3
    lane = iota((768, LANES), 1)

    def gather(source, tiles):
        move = [one_hot(functools.reduce(jnp.logical_or, [at == lane + k * LANES for at in source])) for k in range(tiles)]
        return jnp.concatenate(move, axis=1).astype(BF16)

    rows = jnp.concatenate([part[0:12].reshape(192, LANES) for part in parts], axis=0)
    source = (step * 192 + row * 16 + inner).reshape(768, LANES)
    activated[...] = dot(gather([source], 6), rows).astype(BF16).reshape(8, 2, 48, LANES)

    rows = jnp.concatenate([part[12:26].reshape(224, LANES) for part in parts], axis=0)
    source = (step * 224 + (row + 1) * 16 + inner).reshape(768, LANES)
    other = jnp.where(row == 0, ((step + 3) & 3) * 224 + 13 * 16, ((step + 1) & 3) * 224) + inner
    border = ((row == 0) & (part > 0)) | ((row == 11) & (part < 3))
    other = jnp.where(border, other, -1).reshape(768, LANES)
    input_grad[...] = dot(gather([source, other], 7), rows).astype(BF16).reshape(8, 2, 48, LANES)


def band_kernel(by_out, by_in, forward, backward):
    column = iota((32, 192), 1)
    spread = one_hot(column // 16 % 4 * 8 + column % 8 == iota((32, 192), 0)).astype(BF16)
    wide = dot(by_out[...], spread)
    column = iota((8, 192), 1)
    plane = column // 64 * 2 + column // 8 % 2
    for c in range(3):
        for b in range(3):

            def band(group, target):
                total = jnp.zeros((8, 192), F32)
                for a in range(3):
                    low = (9 * a + 3 * b + c) * 32 + group * 8
                    total = jnp.where(plane == target + a - 1, wide[low : low + 8], total)
                return total

            pieces = [band(group, 2 + x) for group in range(4) for x in range(2)]
            pieces += [band(group, 1) for group in range(4)]
            pieces += [band(group, 4) for group in range(4)]
            forward[b, c * 128 : c * 128 + 128] = jnp.concatenate(pieces, axis=0).astype(BF16)

    column = iota((32, 128), 1)
    channel = jnp.where(column < 64, column // 16 * 8 + column % 8, column % 32)
    wide_in = dot(by_in[...], one_hot(channel == iota((32, 128), 0)).astype(BF16))
    column = iota((8, 128), 1)
    plane_in = jnp.where(column < 64, 2 + column // 8 % 2, jnp.where(column < 96, 1, 4))
    for c in range(3):
        for b in range(3):
            pieces = []
            for group in range(4):
                for x in range(2):
                    total = jnp.zeros((8, 128), F32)
                    for a in range(3):
                        low = (26 - (9 * a + 3 * b + c)) * 32 + group * 8
                        total = jnp.where(plane_in == 1 + x + a, wide_in[low : low + 8], total)
                    pieces.append(total)
            backward[b, c * 64 : c * 64 + 64] = jnp.concatenate(pieces, axis=0).astype(BF16)


def forward_kernel(place, *refs):
    parts, refs = refs[:9], refs[9:]
    forward, activated, upper, grads, field, cots, sides = refs
    member, core = place[0], place[1]

    for s in range(4):
        group = (member + s) & 3
        mine, near, far = parts[(0, 6, 3, 3)[s] :][:3]
        base = 26 if s == 3 else 0
        near_row = pl.multiple_of((1 - core) * 128 + group * 16, 16)
        far_row = pl.multiple_of(core * 128 + group * 16, 16)
        own_row = pl.multiple_of(64 + group * 16, 16)
        for row in range(14):
            here = slice(row * LANES, (row + 1) * LANES)
            field[pl.ds(near_row, 16), here] = near[base + row]
            field[pl.ds(own_row, 16), here] = mine[base + row]
            field[pl.ds(far_row, 16), here] = far[base + row]
        cot_row = pl.multiple_of(group * 16, 16)
        near_cot = pl.multiple_of(64 + (1 - core) * 32 + group * 8, 8)
        far_cot = pl.multiple_of(64 + core * 32 + group * 8, 8)
        for row in range(12):
            here = slice(row * LANES, (row + 1) * LANES)
            cots[pl.ds(cot_row, 16), here] = mine[base + 14 + row].astype(F32)
            wide_near = near[base + 14 + row].astype(F32)
            wide_far = far[base + 14 + row].astype(F32)
            cots[pl.ds(near_cot, 8), here] = jnp.where(core == 0, wide_near[0:8], wide_near[8:16])
            cots[pl.ds(far_cot, 8), here] = jnp.where(core == 0, wide_far[8:16], wide_far[0:8])

    upper[:, 0 : 2 * LANES] = jnp.zeros((128, 2 * LANES), BF16)
    upper[:, 14 * LANES : 16 * LANES] = jnp.zeros((128, 2 * LANES), BF16)
    for pair in range(6):
        low = pair * 2
        total = sum(dot(forward[b], field[:, (low + b) * LANES : (low + b + 2) * LANES]) for b in range(3))
        for side in range(2):
            row = low + side
            here = slice(row * LANES, (row + 1) * LANES)
            cut = total[:, side * LANES : (side + 1) * LANES]
            pre = cut[128:256] + shifted(cut[0:128], 1) + shifted(cut[256:384], -1)
            power = jnp.exp(jnp.minimum(pre, 0.0))
            activated[:, here] = jnp.where(pre[:64] > 0, pre[:64], power[:64] - 1.0).astype(BF16)
            cot = cots[:, here]
            up = jnp.where(pre > 0, cot, cot * power).astype(BF16)
            upper[:, (row + 2) * LANES : (row + 3) * LANES] = up
            wide_up = up[:64].astype(F32)
            sides[0:64, here] = shifted(wide_up, -1).astype(BF16)
            sides[64:128, here] = up[:64]
            sides[128:192, here] = shifted(wide_up, 1).astype(BF16)

    row = iota((192, 256), 0)
    col = iota((192, 256), 1)
    row_plane = row // 64 * 2 + row // 8 % 2
    same = row // 16 % 4 * 8 + row % 8 == col % 32
    row9 = iota((192, 128), 0)
    col9 = iota((192, 128), 1)
    plane9 = row9 // 64 * 2 + row9 // 8 % 2
    same9 = row9 // 16 % 4 * 8 + row9 % 8 == col9 % 32
    eight = jnp.zeros((96, 256), F32)
    ninth = jnp.zeros((32, 128), F32)
    for b in range(3):
        product = lax.dot_general(
            sides[...],
            field[:, b * LANES : (12 + b) * LANES],
            (((1,), (1,)), ((), ())),
            preferred_element_type=F32,
        ).reshape(12, 2, 8, 192)
        for x in range(2):
            part = split(product[:, x].reshape(96, 192))
            pick = same & (col // 32 % 3 == b) & (row_plane == 1 + x + col // 96)
            picked = dot(part, one_hot(pick).astype(BF16))
            eight = eight + (picked[0:96] + picked[96:192] + picked[192:288])
            if b == 2:
                for c in range(3):
                    pick = same9 & (col9 // 32 == c) & (plane9 == 3 + x)
                    rows = [part[k * 96 + c * 32 : k * 96 + c * 32 + 32] for k in range(3)]
                    picked = dot(jnp.concatenate(rows, axis=0), one_hot(pick).astype(BF16))
                    ninth = ninth + (picked[0:32] + picked[32:64] + picked[64:96])
    for c in range(3):
        for half in range(2):
            cut = eight[c * 32 : c * 32 + 32, half * LANES : (half + 1) * LANES]
            grads[(c * 2 + half) * 4 : (c * 2 + half) * 4 + 4] = cut.reshape(4, 8, LANES)
    grads[24:28] = ninth.reshape(4, 8, LANES)
    grads[28:32] = jnp.zeros((4, 8, LANES), F32)


def backward_kernel(place, activated, upper, backward, *refs):
    backs, results = refs[:4], refs[4]
    member = place[0]
    for pair in range(7):
        low = pair * 2
        total = sum(dot(backward[b], upper[:, (low + b) * LANES : (low + b + 2) * LANES]) for b in range(3))
        for side in range(2):
            cut = total[:, side * LANES : (side + 1) * LANES]
            grad = cut[64:128] + shifted(cut[0:64], 1) + shifted(cut[128:192], -1)
            results[:, (low + side) * LANES : (low + side + 1) * LANES] = grad.astype(BF16)

    for step, back in enumerate(backs):
        low = pl.multiple_of(((member + step) & 3) * 16, 16)
        for row in range(12):
            back[row] = activated[pl.ds(low, 16), row * LANES : (row + 1) * LANES]
        for row in range(14):
            back[12 + row] = results[pl.ds(low, 16), row * LANES : (row + 1) * LANES]


def call(kernel, outs, scratch=(), place=False, flops=0, moved=0):
    vmem = pl.BlockSpec(memory_space=pltpu.VMEM)
    smem = pl.BlockSpec(memory_space=pltpu.SMEM)

    def run(*args):
        specs = [vmem] * len(args)
        if place:
            specs[0] = smem
        return pl.pallas_call(
            kernel,
            out_shape=outs,
            in_specs=specs,
            out_specs=jax.tree.map(lambda _: vmem, outs),
            scratch_shapes=scratch,
            compiler_params=pltpu.CompilerParams(vmem_limit_bytes=48 * 1024 * 1024),
            cost_estimate=pl.CostEstimate(flops=flops, bytes_accessed=moved, transcendentals=0),
        )(*args)

    return run


def reshard(parts):
    got = [parts[0], None, None, None]
    for step in (2, 1, 3):
        got[4 - step] = lax.ppermute(parts[step], "chan", [(i, (i + step) % 4) for i in range(4)])
    return got


def body(crops, cotangent, weights):
    place = jnp.stack([lax.axis_index("chan"), lax.axis_index("core")]).astype(jnp.int32)
    piece = jax.ShapeDtypeStruct((26, 16, LANES), BF16)
    packed = call(pack_kernel, (piece,) * 4, place=True, flops=10**9)(place, crops[0], cotangent[0])
    got = reshard(packed)
    chips = lax.axis_size("zlo") * lax.axis_size("y")
    remote = [(2 * i + 1, 2 * i + 2) for i in range(chips - 1)]
    remote += [(j, i) for i, j in remote]
    parts = []
    for mine in (got[0], jnp.concatenate([got[2], got[3]], axis=0), got[1]):
        near = lax.ppermute(mine, "core", [(0, 1), (1, 0)])
        far = lax.ppermute(mine, ("zlo", "y", "core"), remote)
        parts += [mine, near, far]
    by_out = jnp.transpose(weights, (1, 0, 2)).reshape(864, 32)
    by_in = jnp.transpose(weights, (1, 2, 0)).reshape(864, 32)
    forward, backward = call(
        band_kernel,
        (jax.ShapeDtypeStruct((3, 384, 192), BF16), jax.ShapeDtypeStruct((3, 192, 128), BF16)),
        flops=10**9,
    )(by_out, by_in)
    rows = jax.ShapeDtypeStruct((64, 12 * LANES), BF16)
    activated, upper, grads = call(
        forward_kernel,
        (rows, jax.ShapeDtypeStruct((128, 16 * LANES), BF16), jax.ShapeDtypeStruct((32, 8, LANES), F32)),
        [
            pltpu.VMEM((192, 14 * LANES), BF16),
            pltpu.VMEM((128, 12 * LANES), F32),
            pltpu.VMEM((192, 12 * LANES), BF16),
        ],
        place=True,
        flops=3 * 10**9,
    )(place, *parts, forward)
    piece = jax.ShapeDtypeStruct((26, 16, LANES), BF16)
    backs = call(
        backward_kernel,
        (piece,) * 4,
        [pltpu.VMEM((64, 14 * LANES), BF16)],
        place=True,
        flops=2 * 10**9,
    )(place, activated, upper, backward)
    plane = ("y", "core", "batch")
    column = ("zlo", "chan")
    pieces, rest = lax.axis_size(plane), lax.axis_size(column)
    terms = lax.all_to_all(grads.reshape((pieces, -1) + grads.shape[1:]), plane, 0, 0)
    terms, backs = lax.optimization_barrier((terms, backs))
    share = jnp.sum(terms, axis=0)
    terms = lax.all_to_all(jnp.broadcast_to(share, (rest,) + share.shape), column, 0, 0)
    cells = pieces * rest // lax.axis_size("chan") * crops.shape[2] * crops.shape[3] * crops.shape[4]
    share = jnp.sum(terms, axis=0) / jnp.sqrt(jnp.float32(cells))
    whole = lax.all_to_all(jnp.broadcast_to(share, (pieces,) + share.shape), plane, 0, 0).reshape(32, 8, LANES)
    slab = jax.ShapeDtypeStruct((8, 2, 48, LANES), BF16)
    activated, input_grad = call(unpack_kernel, (slab, slab), place=True, flops=10**9)(place, *reshard(backs))
    eight = whole[:24].reshape(3, 2, 4, 8, 4, 32).transpose(2, 3, 1, 4, 0, 5).reshape(32, 8, 3, 32)
    ninth = whole[24:28].reshape(32, 1, 4, 32)[:, :, :3]
    weight_grad = jnp.concatenate([eight, ninth], axis=1).reshape(32, 27, 32)
    return activated[None], input_grad[None], weight_grad


def solution(mesh):
    space, chan, batch = (mesh.shape[name] for name in ("space", "chan", "batch"))
    cut = mesh.devices.reshape(space // 8, 4, 2, chan, batch)
    fine = Mesh(cut, ("zlo", "y", "core", "chan", "batch"))
    spec = P("batch", "chan", ("zlo", "y", "core"), None, None)
    return jax.shard_map(
        body,
        mesh=fine,
        in_specs=(spec, spec, P()),
        out_specs=(spec, spec, P()),
        check_vma=False,
    )
```

```python
import functools

import jax
import jax.numpy as jnp
from jax import lax
from jax.experimental import pallas as pl
from jax.experimental.pallas import tpu as pltpu
from jax.sharding import Mesh, PartitionSpec as P

LANES = 128
F32 = jnp.float32
BF16 = jnp.bfloat16


def iota(shape, dim):
    return lax.broadcasted_iota(jnp.int32, shape, dim)


def one_hot(hit):
    return jnp.where(hit, 1.0, 0.0)


def dot(left, right, **options):
    return jnp.dot(left, right, preferred_element_type=F32, **options)


def split(block):
    high = block.astype(BF16)
    rest = block - high.astype(F32)
    middle = rest.astype(BF16)
    low = (rest - middle.astype(F32)).astype(BF16)
    return jnp.concatenate([high, middle, low], axis=0)


def shifted(block, step):
    moved = pltpu.roll(block, step % LANES, 1)
    lane = iota(block.shape, 1)
    edge = 0 if step == 1 else LANES - 1
    return jnp.where(lane == edge, 0.0, moved)


def pack_kernel(place, crops, cotangent, *outs):
    row = iota((256, LANES), 0)
    lane = iota((256, LANES), 1)
    base = (row & 7) * 96 + (row >> 3 & 1) * 48
    moves = []
    for step in range(4):
        part = (place[0] + step) & 3
        y = (row >> 4) + (12 * part - 2)
        source = jnp.where((y >= 0) & (y < 48), base + y, -1)
        tiles = [one_hot(source == lane + k * LANES).astype(BF16) for k in range(6)]
        moves.append(jnp.concatenate(tiles, axis=1))
    both = jnp.concatenate([crops[...].reshape(768, LANES), cotangent[...].reshape(768, LANES)], axis=1)
    for move, out in zip(moves, outs):
        moved = dot(move, both).astype(BF16).reshape(16, 16, 2 * LANES)
        out[0:14] = moved[1:15, :, :LANES]
        out[14:26] = moved[2:14, :, LANES:]


def unpack_kernel(place, *refs):
    parts, (activated, input_grad) = refs[:4], refs[4:]
    outer = iota((16, 48, LANES), 0)
    y = iota((16, 48, LANES), 1)
    part = (y >= 12).astype(jnp.int32) + (y >= 24).astype(jnp.int32) + (y >= 36).astype(jnp.int32)
    row = y - 12 * part
    inner = (outer & 1) * 8 + (outer >> 1)
    step = (part + 4 - place[0]) & 3
    lane = iota((768, LANES), 1)

    def gather(source, tiles):
        move = [one_hot(functools.reduce(jnp.logical_or, [at == lane + k * LANES for at in source])) for k in range(tiles)]
        return jnp.concatenate(move, axis=1).astype(BF16)

    rows = jnp.concatenate([part[0:12].reshape(192, LANES) for part in parts], axis=0)
    source = (step * 192 + row * 16 + inner).reshape(768, LANES)
    activated[...] = dot(gather([source], 6), rows).astype(BF16).reshape(8, 2, 48, LANES)

    rows = jnp.concatenate([part[12:26].reshape(224, LANES) for part in parts], axis=0)
    source = (step * 224 + (row + 1) * 16 + inner).reshape(768, LANES)
    other = jnp.where(row == 0, ((step + 3) & 3) * 224 + 13 * 16, ((step + 1) & 3) * 224) + inner
    border = ((row == 0) & (part > 0)) | ((row == 11) & (part < 3))
    other = jnp.where(border, other, -1).reshape(768, LANES)
    input_grad[...] = dot(gather([source, other], 7), rows).astype(BF16).reshape(8, 2, 48, LANES)


def band_kernel(by_out, by_in, forward, backward):
    column = iota((32, 192), 1)
    spread = one_hot(column // 16 % 4 * 8 + column % 8 == iota((32, 192), 0)).astype(BF16)
    wide = dot(by_out[...], spread)
    column = iota((8, 192), 1)
    plane = column // 64 * 2 + column // 8 % 2
    for c in range(3):
        for b in range(3):

            def band(group, target):
                total = jnp.zeros((8, 192), F32)
                for a in range(3):
                    low = (9 * a + 3 * b + c) * 32 + group * 8
                    total = jnp.where(plane == target + a - 1, wide[low : low + 8], total)
                return total

            pieces = [band(group, 2 + x) for group in range(4) for x in range(2)]
            pieces += [band(group, 1) for group in range(4)]
            pieces += [band(group, 4) for group in range(4)]
            forward[b, c * 128 : c * 128 + 128] = jnp.concatenate(pieces, axis=0).astype(BF16)

    column = iota((32, 128), 1)
    channel = jnp.where(column < 64, column // 16 * 8 + column % 8, column % 32)
    wide_in = dot(by_in[...], one_hot(channel == iota((32, 128), 0)).astype(BF16))
    column = iota((8, 128), 1)
    plane_in = jnp.where(column < 64, 2 + column // 8 % 2, jnp.where(column < 96, 1, 4))
    for c in range(3):
        for b in range(3):
            pieces = []
            for group in range(4):
                for x in range(2):
                    total = jnp.zeros((8, 128), F32)
                    for a in range(3):
                        low = (26 - (9 * a + 3 * b + c)) * 32 + group * 8
                        total = jnp.where(plane_in == 1 + x + a, wide_in[low : low + 8], total)
                    pieces.append(total)
            backward[b, c * 64 : c * 64 + 64] = jnp.concatenate(pieces, axis=0).astype(BF16)


def forward_kernel(place, *refs):
    parts, refs = refs[:6], refs[6:]
    forward, activated, upper, grads, field, cots, sides = refs
    member, core = place[0], place[1]

    for s in range(4):
        group = (member + s) & 3
        mine, near, far = parts[(0, 3, 3, 3)[s] :][:3]
        base = (0, 52, 0, 26)[s]
        near_row = pl.multiple_of((1 - core) * 128 + group * 16, 16)
        far_row = pl.multiple_of(core * 128 + group * 16, 16)
        own_row = pl.multiple_of(64 + group * 16, 16)
        for row in range(14):
            here = slice(row * LANES, (row + 1) * LANES)
            field[pl.ds(near_row, 16), here] = near[base + row]
            field[pl.ds(own_row, 16), here] = mine[base + row]
            field[pl.ds(far_row, 16), here] = far[base + row]
        cot_row = pl.multiple_of(group * 16, 16)
        near_cot = pl.multiple_of(64 + (1 - core) * 32 + group * 8, 8)
        far_cot = pl.multiple_of(64 + core * 32 + group * 8, 8)
        for row in range(12):
            here = slice(row * LANES, (row + 1) * LANES)
            cots[pl.ds(cot_row, 16), here] = mine[base + 14 + row].astype(F32)
            wide_near = near[base + 14 + row].astype(F32)
            wide_far = far[base + 14 + row].astype(F32)
            cots[pl.ds(near_cot, 8), here] = jnp.where(core == 0, wide_near[0:8], wide_near[8:16])
            cots[pl.ds(far_cot, 8), here] = jnp.where(core == 0, wide_far[8:16], wide_far[0:8])

    upper[:, 0 : 2 * LANES] = jnp.zeros((128, 2 * LANES), BF16)
    upper[:, 14 * LANES : 16 * LANES] = jnp.zeros((128, 2 * LANES), BF16)
    for pair in range(6):
        low = pair * 2
        total = sum(dot(forward[b], field[:, (low + b) * LANES : (low + b + 2) * LANES]) for b in range(3))
        for side in range(2):
            row = low + side
            here = slice(row * LANES, (row + 1) * LANES)
            cut = total[:, side * LANES : (side + 1) * LANES]
            pre = cut[128:256] + shifted(cut[0:128], 1) + shifted(cut[256:384], -1)
            power = jnp.exp(jnp.minimum(pre, 0.0))
            activated[:, here] = jnp.where(pre[:64] > 0, pre[:64], power[:64] - 1.0).astype(BF16)
            cot = cots[:, here]
            up = jnp.where(pre > 0, cot, cot * power).astype(BF16)
            upper[:, (row + 2) * LANES : (row + 3) * LANES] = up
            wide_up = up[:64].astype(F32)
            sides[0:64, here] = shifted(wide_up, -1).astype(BF16)
            sides[64:128, here] = up[:64]
            sides[128:192, here] = shifted(wide_up, 1).astype(BF16)

    row = iota((192, 256), 0)
    col = iota((192, 256), 1)
    row_plane = row // 64 * 2 + row // 8 % 2
    same = row // 16 % 4 * 8 + row % 8 == col % 32
    row9 = iota((192, 128), 0)
    col9 = iota((192, 128), 1)
    plane9 = row9 // 64 * 2 + row9 // 8 % 2
    same9 = row9 // 16 % 4 * 8 + row9 % 8 == col9 % 32
    eight = jnp.zeros((96, 256), F32)
    ninth = jnp.zeros((32, 128), F32)
    for b in range(3):
        product = lax.dot_general(
            sides[...],
            field[:, b * LANES : (12 + b) * LANES],
            (((1,), (1,)), ((), ())),
            preferred_element_type=F32,
        ).reshape(12, 2, 8, 192)
        for x in range(2):
            part = split(product[:, x].reshape(96, 192))
            pick = same & (col // 32 % 3 == b) & (row_plane == 1 + x + col // 96)
            picked = dot(part, one_hot(pick).astype(BF16))
            eight = eight + (picked[0:96] + picked[96:192] + picked[192:288])
            if b == 2:
                for c in range(3):
                    pick = same9 & (col9 // 32 == c) & (plane9 == 3 + x)
                    rows = [part[k * 96 + c * 32 : k * 96 + c * 32 + 32] for k in range(3)]
                    picked = dot(jnp.concatenate(rows, axis=0), one_hot(pick).astype(BF16))
                    ninth = ninth + (picked[0:32] + picked[32:64] + picked[64:96])
    for c in range(3):
        for half in range(2):
            cut = eight[c * 32 : c * 32 + 32, half * LANES : (half + 1) * LANES]
            grads[(c * 2 + half) * 4 : (c * 2 + half) * 4 + 4] = cut.reshape(4, 8, LANES)
    grads[24:28] = ninth.reshape(4, 8, LANES)
    grads[28:32] = jnp.zeros((4, 8, LANES), F32)


def backward_kernel(place, activated, upper, backward, *refs):
    backs, results = refs[:4], refs[4]
    member = place[0]
    for pair in range(7):
        low = pair * 2
        total = sum(dot(backward[b], upper[:, (low + b) * LANES : (low + b + 2) * LANES]) for b in range(3))
        for side in range(2):
            cut = total[:, side * LANES : (side + 1) * LANES]
            grad = cut[64:128] + shifted(cut[0:64], 1) + shifted(cut[128:192], -1)
            results[:, (low + side) * LANES : (low + side + 1) * LANES] = grad.astype(BF16)

    for step, back in enumerate(backs):
        low = pl.multiple_of(((member + step) & 3) * 16, 16)
        for row in range(12):
            back[row] = activated[pl.ds(low, 16), row * LANES : (row + 1) * LANES]
        for row in range(14):
            back[12 + row] = results[pl.ds(low, 16), row * LANES : (row + 1) * LANES]


def call(kernel, outs, scratch=(), place=False, flops=0, moved=0):
    vmem = pl.BlockSpec(memory_space=pltpu.VMEM)
    smem = pl.BlockSpec(memory_space=pltpu.SMEM)

    def run(*args):
        specs = [vmem] * len(args)
        if place:
            specs[0] = smem
        return pl.pallas_call(
            kernel,
            out_shape=outs,
            in_specs=specs,
            out_specs=jax.tree.map(lambda _: vmem, outs),
            scratch_shapes=scratch,
            compiler_params=pltpu.CompilerParams(vmem_limit_bytes=48 * 1024 * 1024),
            cost_estimate=pl.CostEstimate(flops=flops, bytes_accessed=moved, transcendentals=0),
        )(*args)

    return run


def reshard(parts):
    got = [parts[0], None, None, None]
    for step in (1, 3, 2):
        got[4 - step] = lax.ppermute(parts[step], "chan", [(i, (i + step) % 4) for i in range(4)])
    return got


def body(crops, cotangent, weights):
    place = jnp.stack([lax.axis_index("chan"), lax.axis_index("core")]).astype(jnp.int32)
    piece = jax.ShapeDtypeStruct((26, 16, LANES), BF16)
    packed = call(pack_kernel, (piece,) * 4, place=True, flops=10**9)(place, crops[0], cotangent[0])
    got = reshard(packed)
    chips = lax.axis_size("zlo") * lax.axis_size("y")
    remote = [(2 * i + 1, 2 * i + 2) for i in range(chips - 1)]
    remote += [(j, i) for i, j in remote]
    parts = []
    for mine in (got[0], None):
        if mine is None:
            *parts, a, b, c = lax.optimization_barrier((*parts, got[2], got[3], got[1]))
            mine = jnp.concatenate([a, b, c], axis=0)
        near = lax.ppermute(mine, "core", [(0, 1), (1, 0)])
        far = lax.ppermute(mine, ("zlo", "y", "core"), remote)
        parts += [mine, near, far]
    by_out = jnp.transpose(weights, (1, 0, 2)).reshape(864, 32)
    by_in = jnp.transpose(weights, (1, 2, 0)).reshape(864, 32)
    forward, backward = call(
        band_kernel,
        (jax.ShapeDtypeStruct((3, 384, 192), BF16), jax.ShapeDtypeStruct((3, 192, 128), BF16)),
        flops=10**9,
    )(by_out, by_in)
    rows = jax.ShapeDtypeStruct((64, 12 * LANES), BF16)
    activated, upper, grads = call(
        forward_kernel,
        (rows, jax.ShapeDtypeStruct((128, 16 * LANES), BF16), jax.ShapeDtypeStruct((32, 8, LANES), F32)),
        [
            pltpu.VMEM((192, 14 * LANES), BF16),
            pltpu.VMEM((128, 12 * LANES), F32),
            pltpu.VMEM((192, 12 * LANES), BF16),
        ],
        place=True,
        flops=3 * 10**9,
    )(place, *parts, forward)
    piece = jax.ShapeDtypeStruct((26, 16, LANES), BF16)
    backs = call(
        backward_kernel,
        (piece,) * 4,
        [pltpu.VMEM((64, 14 * LANES), BF16)],
        place=True,
        flops=2 * 10**9,
    )(place, activated, upper, backward)
    plane = ("y", "core", "batch")
    column = ("zlo", "chan")
    pieces, rest = lax.axis_size(plane), lax.axis_size(column)
    terms = lax.all_to_all(grads.reshape((pieces, -1) + grads.shape[1:]), plane, 0, 0)
    terms, backs = lax.optimization_barrier((terms, backs))
    share = jnp.sum(terms, axis=0)
    terms = lax.all_to_all(jnp.broadcast_to(share, (rest,) + share.shape), column, 0, 0)
    cells = pieces * rest // lax.axis_size("chan") * crops.shape[2] * crops.shape[3] * crops.shape[4]
    share = jnp.sum(terms, axis=0) / jnp.sqrt(jnp.float32(cells))
    whole = lax.all_to_all(jnp.broadcast_to(share, (pieces,) + share.shape), plane, 0, 0).reshape(32, 8, LANES)
    slab = jax.ShapeDtypeStruct((8, 2, 48, LANES), BF16)
    activated, input_grad = call(unpack_kernel, (slab, slab), place=True, flops=10**9)(place, *reshard(backs))
    eight = whole[:24].reshape(3, 2, 4, 8, 4, 32).transpose(2, 3, 1, 4, 0, 5).reshape(32, 8, 3, 32)
    ninth = whole[24:28].reshape(32, 1, 4, 32)[:, :, :3]
    weight_grad = jnp.concatenate([eight, ninth], axis=1).reshape(32, 27, 32)
    return activated[None], input_grad[None], weight_grad


def solution(mesh):
    space, chan, batch = (mesh.shape[name] for name in ("space", "chan", "batch"))
    cut = mesh.devices.reshape(space // 8, 4, 2, chan, batch)
    fine = Mesh(cut, ("zlo", "y", "core", "chan", "batch"))
    spec = P("batch", "chan", ("zlo", "y", "core"), None, None)
    return jax.shard_map(
        body,
        mesh=fine,
        in_specs=(spec, spec, P()),
        out_specs=(spec, spec, P()),
        check_vma=False,
    )
```

```python
import functools

import jax
import jax.numpy as jnp
from jax import lax
from jax.experimental import pallas as pl
from jax.experimental.pallas import tpu as pltpu
from jax.sharding import Mesh, PartitionSpec as P

LANES = 128
F32 = jnp.float32
BF16 = jnp.bfloat16


def iota(shape, dim):
    return lax.broadcasted_iota(jnp.int32, shape, dim)


def one_hot(hit):
    return jnp.where(hit, 1.0, 0.0)


def dot(left, right, **options):
    return jnp.dot(left, right, preferred_element_type=F32, **options)


def split(block):
    high = block.astype(BF16)
    rest = block - high.astype(F32)
    middle = rest.astype(BF16)
    low = (rest - middle.astype(F32)).astype(BF16)
    return jnp.concatenate([high, middle, low], axis=0)


def shifted(block, step):
    moved = pltpu.roll(block, step % LANES, 1)
    lane = iota(block.shape, 1)
    edge = 0 if step == 1 else LANES - 1
    return jnp.where(lane == edge, 0.0, moved)


def pack_kernel(place, crops, cotangent, *outs):
    row = iota((256, LANES), 0)
    lane = iota((256, LANES), 1)
    base = (row & 7) * 96 + (row >> 3 & 1) * 48
    moves = []
    for step in range(4):
        part = (place[0] + step) & 3
        y = (row >> 4) + (12 * part - 2)
        source = jnp.where((y >= 0) & (y < 48), base + y, -1)
        tiles = [one_hot(source == lane + k * LANES).astype(BF16) for k in range(6)]
        moves.append(jnp.concatenate(tiles, axis=1))
    both = jnp.concatenate([crops[...].reshape(768, LANES), cotangent[...].reshape(768, LANES)], axis=1)
    for move, out in zip(moves, outs):
        moved = dot(move, both).astype(BF16).reshape(16, 16, 2 * LANES)
        out[0:14] = moved[1:15, :, :LANES]
        out[14:26] = moved[2:14, :, LANES:]


def moves_kernel(place, plain, summed):
    outer = iota((16, 48, LANES), 0)
    y = iota((16, 48, LANES), 1)
    part = (y >= 12).astype(jnp.int32) + (y >= 24).astype(jnp.int32) + (y >= 36).astype(jnp.int32)
    row = y - 12 * part
    inner = (outer & 1) * 8 + (outer >> 1)
    step = (part + 4 - place[0]) & 3
    lane = iota((768, LANES), 1)

    def gather(source, tiles):
        move = [one_hot(functools.reduce(jnp.logical_or, [at == lane + k * LANES for at in source])) for k in range(tiles)]
        return jnp.concatenate(move, axis=1).astype(BF16)

    source = (step * 192 + row * 16 + inner).reshape(768, LANES)
    plain[...] = gather([source], 6)
    source = (step * 224 + (row + 1) * 16 + inner).reshape(768, LANES)
    other = jnp.where(row == 0, ((step + 3) & 3) * 224 + 13 * 16, ((step + 1) & 3) * 224) + inner
    border = ((row == 0) & (part > 0)) | ((row == 11) & (part < 3))
    other = jnp.where(border, other, -1).reshape(768, LANES)
    summed[...] = gather([source, other], 7)


def unpack_kernel(plain, summed, *refs):
    mine, opposite, *sides = refs[:4]
    parts, (activated, input_grad) = (mine, sides[0], opposite, sides[1]), refs[4:]
    rows = jnp.concatenate([part[0:12].reshape(192, LANES) for part in parts], axis=0)
    activated[...] = dot(plain[...], rows).astype(BF16).reshape(8, 2, 48, LANES)
    rows = jnp.concatenate([part[12:26].reshape(224, LANES) for part in parts], axis=0)
    input_grad[...] = dot(summed[...], rows).astype(BF16).reshape(8, 2, 48, LANES)


def band_kernel(by_out, by_in, forward, backward):
    column = iota((32, 192), 1)
    spread = one_hot(column // 16 % 4 * 8 + column % 8 == iota((32, 192), 0)).astype(BF16)
    wide = dot(by_out[...], spread)
    column = iota((8, 192), 1)
    plane = column // 64 * 2 + column // 8 % 2
    for c in range(3):
        for b in range(3):

            def band(group, target):
                total = jnp.zeros((8, 192), F32)
                for a in range(3):
                    low = (9 * a + 3 * b + c) * 32 + group * 8
                    total = jnp.where(plane == target + a - 1, wide[low : low + 8], total)
                return total

            pieces = [band(group, 2 + x) for group in range(4) for x in range(2)]
            pieces += [band(group, 1) for group in range(4)]
            pieces += [band(group, 4) for group in range(4)]
            forward[b, c * 128 : c * 128 + 128] = jnp.concatenate(pieces, axis=0).astype(BF16)

    column = iota((32, 128), 1)
    channel = jnp.where(column < 64, column // 16 * 8 + column % 8, column % 32)
    wide_in = dot(by_in[...], one_hot(channel == iota((32, 128), 0)).astype(BF16))
    column = iota((8, 128), 1)
    plane_in = jnp.where(column < 64, 2 + column // 8 % 2, jnp.where(column < 96, 1, 4))
    for c in range(3):
        for b in range(3):
            pieces = []
            for group in range(4):
                for x in range(2):
                    total = jnp.zeros((8, 128), F32)
                    for a in range(3):
                        low = (26 - (9 * a + 3 * b + c)) * 32 + group * 8
                        total = jnp.where(plane_in == 1 + x + a, wide_in[low : low + 8], total)
                    pieces.append(total)
            backward[b, c * 64 : c * 64 + 64] = jnp.concatenate(pieces, axis=0).astype(BF16)


def forward_kernel(place, *refs):
    parts, refs = refs[:6], refs[6:]
    forward, activated, upper, grads, field, cots, sides = refs
    member, core = place[0], place[1]

    for s in range(4):
        group = (member + s) & 3
        mine, near, far = parts[(0, 3, 3, 3)[s] :][:3]
        base = (0, 52, 0, 26)[s]
        near_row = pl.multiple_of((1 - core) * 128 + group * 16, 16)
        far_row = pl.multiple_of(core * 128 + group * 16, 16)
        own_row = pl.multiple_of(64 + group * 16, 16)
        for row in range(14):
            here = slice(row * LANES, (row + 1) * LANES)
            field[pl.ds(near_row, 16), here] = near[base + row]
            field[pl.ds(own_row, 16), here] = mine[base + row]
            field[pl.ds(far_row, 16), here] = far[base + row]
        cot_row = pl.multiple_of(group * 16, 16)
        near_cot = pl.multiple_of(64 + (1 - core) * 32 + group * 8, 8)
        far_cot = pl.multiple_of(64 + core * 32 + group * 8, 8)
        for row in range(12):
            here = slice(row * LANES, (row + 1) * LANES)
            cots[pl.ds(cot_row, 16), here] = mine[base + 14 + row].astype(F32)
            wide_near = near[base + 14 + row].astype(F32)
            wide_far = far[base + 14 + row].astype(F32)
            cots[pl.ds(near_cot, 8), here] = jnp.where(core == 0, wide_near[0:8], wide_near[8:16])
            cots[pl.ds(far_cot, 8), here] = jnp.where(core == 0, wide_far[8:16], wide_far[0:8])

    upper[:, 0 : 2 * LANES] = jnp.zeros((128, 2 * LANES), BF16)
    upper[:, 14 * LANES : 16 * LANES] = jnp.zeros((128, 2 * LANES), BF16)
    for pair in range(6):
        low = pair * 2
        total = sum(dot(forward[b], field[:, (low + b) * LANES : (low + b + 2) * LANES]) for b in range(3))
        for side in range(2):
            row = low + side
            here = slice(row * LANES, (row + 1) * LANES)
            cut = total[:, side * LANES : (side + 1) * LANES]
            pre = cut[128:256] + shifted(cut[0:128], 1) + shifted(cut[256:384], -1)
            power = jnp.exp(jnp.minimum(pre, 0.0))
            activated[:, here] = jnp.where(pre[:64] > 0, pre[:64], power[:64] - 1.0).astype(BF16)
            cot = cots[:, here]
            up = jnp.where(pre > 0, cot, cot * power).astype(BF16)
            upper[:, (row + 2) * LANES : (row + 3) * LANES] = up
            wide_up = up[:64].astype(F32)
            sides[0:64, here] = shifted(wide_up, -1).astype(BF16)
            sides[64:128, here] = up[:64]
            sides[128:192, here] = shifted(wide_up, 1).astype(BF16)

    row = iota((192, 256), 0)
    col = iota((192, 256), 1)
    row_plane = row // 64 * 2 + row // 8 % 2
    same = row // 16 % 4 * 8 + row % 8 == col % 32
    row9 = iota((192, 128), 0)
    col9 = iota((192, 128), 1)
    plane9 = row9 // 64 * 2 + row9 // 8 % 2
    same9 = row9 // 16 % 4 * 8 + row9 % 8 == col9 % 32
    eight = jnp.zeros((96, 256), F32)
    ninth = jnp.zeros((32, 128), F32)
    for b in range(3):
        product = lax.dot_general(
            sides[...],
            field[:, b * LANES : (12 + b) * LANES],
            (((1,), (1,)), ((), ())),
            preferred_element_type=F32,
        ).reshape(12, 2, 8, 192)
        for x in range(2):
            part = split(product[:, x].reshape(96, 192))
            pick = same & (col // 32 % 3 == b) & (row_plane == 1 + x + col // 96)
            picked = dot(part, one_hot(pick).astype(BF16))
            eight = eight + (picked[0:96] + picked[96:192] + picked[192:288])
            if b == 2:
                for c in range(3):
                    pick = same9 & (col9 // 32 == c) & (plane9 == 3 + x)
                    rows = [part[k * 96 + c * 32 : k * 96 + c * 32 + 32] for k in range(3)]
                    picked = dot(jnp.concatenate(rows, axis=0), one_hot(pick).astype(BF16))
                    ninth = ninth + (picked[0:32] + picked[32:64] + picked[64:96])
    for c in range(3):
        for half in range(2):
            cut = eight[c * 32 : c * 32 + 32, half * LANES : (half + 1) * LANES]
            grads[(c * 2 + half) * 4 : (c * 2 + half) * 4 + 4] = cut.reshape(4, 8, LANES)
    grads[24:28] = ninth.reshape(4, 8, LANES)
    grads[28:32] = jnp.zeros((4, 8, LANES), F32)


def backward_kernel(place, activated, upper, backward, *refs):
    backs, results = refs[:4], refs[4]
    member = place[0]
    for pair in range(7):
        low = pair * 2
        total = sum(dot(backward[b], upper[:, (low + b) * LANES : (low + b + 2) * LANES]) for b in range(3))
        for side in range(2):
            cut = total[:, side * LANES : (side + 1) * LANES]
            grad = cut[64:128] + shifted(cut[0:64], 1) + shifted(cut[128:192], -1)
            results[:, (low + side) * LANES : (low + side + 1) * LANES] = grad.astype(BF16)

    for step, back in enumerate(backs):
        low = pl.multiple_of(((member + step) & 3) * 16, 16)
        for row in range(12):
            back[row] = activated[pl.ds(low, 16), row * LANES : (row + 1) * LANES]
        for row in range(14):
            back[12 + row] = results[pl.ds(low, 16), row * LANES : (row + 1) * LANES]


def call(kernel, outs, scratch=(), place=False, flops=0, moved=0):
    vmem = pl.BlockSpec(memory_space=pltpu.VMEM)
    smem = pl.BlockSpec(memory_space=pltpu.SMEM)

    def run(*args):
        specs = [vmem] * len(args)
        if place:
            specs[0] = smem
        return pl.pallas_call(
            kernel,
            out_shape=outs,
            in_specs=specs,
            out_specs=jax.tree.map(lambda _: vmem, outs),
            scratch_shapes=scratch,
            compiler_params=pltpu.CompilerParams(vmem_limit_bytes=48 * 1024 * 1024),
            cost_estimate=pl.CostEstimate(flops=flops, bytes_accessed=moved, transcendentals=0),
        )(*args)

    return run


def reshard(parts):
    got = [parts[0], None, None, None]
    for step in (1, 3, 2):
        got[4 - step] = lax.ppermute(parts[step], "chan", [(i, (i + step) % 4) for i in range(4)])
    return got


def body(crops, cotangent, weights):
    place = jnp.stack([lax.axis_index("chan"), lax.axis_index("core")]).astype(jnp.int32)
    piece = jax.ShapeDtypeStruct((26, 16, LANES), BF16)
    packed = call(pack_kernel, (piece,) * 4, place=True, flops=10**9)(place, crops[0], cotangent[0])
    got = reshard(packed)
    chips = lax.axis_size("zlo") * lax.axis_size("y")
    remote = [(2 * i + 1, 2 * i + 2) for i in range(chips - 1)]
    remote += [(j, i) for i, j in remote]
    parts = []
    for mine in (got[0], None):
        if mine is None:
            *parts, a, b, c = lax.optimization_barrier((*parts, got[2], got[3], got[1]))
            mine = jnp.concatenate([a, b, c], axis=0)
        near = lax.ppermute(mine, "core", [(0, 1), (1, 0)])
        far = lax.ppermute(mine, ("zlo", "y", "core"), remote)
        parts += [mine, near, far]
    by_out = jnp.transpose(weights, (1, 0, 2)).reshape(864, 32)
    by_in = jnp.transpose(weights, (1, 2, 0)).reshape(864, 32)
    forward, backward = call(
        band_kernel,
        (jax.ShapeDtypeStruct((3, 384, 192), BF16), jax.ShapeDtypeStruct((3, 192, 128), BF16)),
        flops=10**9,
    )(by_out, by_in)
    rows = jax.ShapeDtypeStruct((64, 12 * LANES), BF16)
    activated, upper, grads = call(
        forward_kernel,
        (rows, jax.ShapeDtypeStruct((128, 16 * LANES), BF16), jax.ShapeDtypeStruct((32, 8, LANES), F32)),
        [
            pltpu.VMEM((192, 14 * LANES), BF16),
            pltpu.VMEM((128, 12 * LANES), F32),
            pltpu.VMEM((192, 12 * LANES), BF16),
        ],
        place=True,
        flops=3 * 10**9,
    )(place, *parts, forward)
    piece = jax.ShapeDtypeStruct((26, 16, LANES), BF16)
    backs = call(
        backward_kernel,
        (piece,) * 4,
        [pltpu.VMEM((64, 14 * LANES), BF16)],
        place=True,
        flops=2 * 10**9,
    )(place, activated, upper, backward)
    plane = ("y", "core", "batch")
    column = ("zlo", "chan")
    pieces, rest = lax.axis_size(plane), lax.axis_size(column)
    terms = lax.all_to_all(grads.reshape((pieces, -1) + grads.shape[1:]), plane, 0, 0)
    terms, backs = lax.optimization_barrier((terms, backs))
    share = jnp.sum(terms, axis=0)
    terms = lax.all_to_all(jnp.broadcast_to(share, (rest,) + share.shape), column, 0, 0)
    cells = pieces * rest // lax.axis_size("chan") * crops.shape[2] * crops.shape[3] * crops.shape[4]
    share = jnp.sum(terms, axis=0) / jnp.sqrt(jnp.float32(cells))
    whole = lax.all_to_all(jnp.broadcast_to(share, (pieces,) + share.shape), plane, 0, 0).reshape(32, 8, LANES)
    slab = jax.ShapeDtypeStruct((8, 2, 48, LANES), BF16)
    moves = call(
        moves_kernel,
        (jax.ShapeDtypeStruct((768, 768), BF16), jax.ShapeDtypeStruct((768, 896), BF16)),
        place=True,
        flops=10**9,
    )(place)
    got = reshard(backs)
    activated, input_grad = call(unpack_kernel, (slab, slab), flops=10**9)(*moves, got[0], got[2], got[1], got[3])
    eight = whole[:24].reshape(3, 2, 4, 8, 4, 32).transpose(2, 3, 1, 4, 0, 5).reshape(32, 8, 3, 32)
    ninth = whole[24:28].reshape(32, 1, 4, 32)[:, :, :3]
    weight_grad = jnp.concatenate([eight, ninth], axis=1).reshape(32, 27, 32)
    return activated[None], input_grad[None], weight_grad


def solution(mesh):
    space, chan, batch = (mesh.shape[name] for name in ("space", "chan", "batch"))
    cut = mesh.devices.reshape(space // 8, 4, 2, chan, batch)
    fine = Mesh(cut, ("zlo", "y", "core", "chan", "batch"))
    spec = P("batch", "chan", ("zlo", "y", "core"), None, None)
    return jax.shard_map(
        body,
        mesh=fine,
        in_specs=(spec, spec, P()),
        out_specs=(spec, spec, P()),
        check_vma=False,
    )
```

```python
import functools

import jax
import jax.numpy as jnp
from jax import lax
from jax.experimental import pallas as pl
from jax.experimental.pallas import tpu as pltpu
from jax.sharding import Mesh, PartitionSpec as P

LANES = 128
F32 = jnp.float32
BF16 = jnp.bfloat16


def iota(shape, dim):
    return lax.broadcasted_iota(jnp.int32, shape, dim)


def one_hot(hit):
    return jnp.where(hit, 1.0, 0.0)


def dot(left, right, **options):
    return jnp.dot(left, right, preferred_element_type=F32, **options)


def split(block):
    high = block.astype(BF16)
    rest = block - high.astype(F32)
    middle = rest.astype(BF16)
    low = (rest - middle.astype(F32)).astype(BF16)
    return jnp.concatenate([high, middle, low], axis=0)


def shifted(block, step):
    moved = pltpu.roll(block, step % LANES, 1)
    lane = iota(block.shape, 1)
    edge = 0 if step == 1 else LANES - 1
    return jnp.where(lane == edge, 0.0, moved)


def pack_kernel(place, crops, cotangent, *outs):
    row = iota((224, LANES), 0)
    lane = iota((224, LANES), 1)
    base = (row & 7) * 96 + (row >> 3 & 1) * 48
    moves = []
    for step in range(4):
        part = (place[0] + step) & 3
        y = (row >> 4) + (12 * part - 1)
        source = jnp.where((y >= 0) & (y < 48), base + y, -1)
        tiles = [one_hot(source == lane + k * LANES).astype(BF16) for k in range(6)]
        moves.append(jnp.concatenate(tiles, axis=1))
    both = jnp.concatenate([crops[...].reshape(768, LANES), cotangent[...].reshape(768, LANES)], axis=1)
    for move, out in zip(moves, outs):
        moved = dot(move, both).astype(BF16).reshape(14, 16, 2 * LANES)
        out[0:14] = moved[:, :, :LANES]
        out[14:26] = moved[1:13, :, LANES:]


def moves_kernel(place, plain, summed):
    outer = iota((16, 48, LANES), 0)
    y = iota((16, 48, LANES), 1)
    part = (y >= 12).astype(jnp.int32) + (y >= 24).astype(jnp.int32) + (y >= 36).astype(jnp.int32)
    row = y - 12 * part
    inner = (outer & 1) * 8 + (outer >> 1)
    step = (part + 4 - place[0]) & 3
    lane = iota((768, LANES), 1)

    def gather(source, tiles):
        move = [one_hot(functools.reduce(jnp.logical_or, [at == lane + k * LANES for at in source])) for k in range(tiles)]
        return jnp.concatenate(move, axis=1).astype(BF16)

    source = (step * 192 + row * 16 + inner).reshape(768, LANES)
    plain[...] = gather([source], 6)
    source = (step * 224 + (row + 1) * 16 + inner).reshape(768, LANES)
    other = jnp.where(row == 0, ((step + 3) & 3) * 224 + 13 * 16, ((step + 1) & 3) * 224) + inner
    border = ((row == 0) & (part > 0)) | ((row == 11) & (part < 3))
    other = jnp.where(border, other, -1).reshape(768, LANES)
    summed[...] = gather([source, other], 7)


def unpack_kernel(plain, summed, *refs):
    mine, opposite, *sides = refs[:4]
    parts, (activated, input_grad) = (mine, sides[0], opposite, sides[1]), refs[4:]
    rows = jnp.concatenate([part[0:12].reshape(192, LANES) for part in parts], axis=0)
    activated[...] = dot(plain[...], rows).astype(BF16).reshape(8, 2, 48, LANES)
    rows = jnp.concatenate([part[12:26].reshape(224, LANES) for part in parts], axis=0)
    input_grad[...] = dot(summed[...], rows).astype(BF16).reshape(8, 2, 48, LANES)


def band_kernel(by_out, by_in, forward, backward):
    column = iota((32, 192), 1)
    spread = one_hot(column // 16 % 4 * 8 + column % 8 == iota((32, 192), 0)).astype(BF16)
    wide = dot(by_out[...], spread)
    column = iota((8, 192), 1)
    plane = column // 64 * 2 + column // 8 % 2
    for c in range(3):
        for b in range(3):

            def band(group, target):
                total = jnp.zeros((8, 192), F32)
                for a in range(3):
                    low = (9 * a + 3 * b + c) * 32 + group * 8
                    total = jnp.where(plane == target + a - 1, wide[low : low + 8], total)
                return total

            pieces = [band(group, 2 + x) for group in range(4) for x in range(2)]
            pieces += [band(group, 1) for group in range(4)]
            pieces += [band(group, 4) for group in range(4)]
            forward[b, c * 128 : c * 128 + 128] = jnp.concatenate(pieces, axis=0).astype(BF16)

    column = iota((32, 128), 1)
    channel = jnp.where(column < 64, column // 16 * 8 + column % 8, column % 32)
    wide_in = dot(by_in[...], one_hot(channel == iota((32, 128), 0)).astype(BF16))
    column = iota((8, 128), 1)
    plane_in = jnp.where(column < 64, 2 + column // 8 % 2, jnp.where(column < 96, 1, 4))
    for c in range(3):
        for b in range(3):
            pieces = []
            for group in range(4):
                for x in range(2):
                    total = jnp.zeros((8, 128), F32)
                    for a in range(3):
                        low = (26 - (9 * a + 3 * b + c)) * 32 + group * 8
                        total = jnp.where(plane_in == 1 + x + a, wide_in[low : low + 8], total)
                    pieces.append(total)
            backward[b, c * 64 : c * 64 + 64] = jnp.concatenate(pieces, axis=0).astype(BF16)


def forward_kernel(place, *refs):
    parts, refs = refs[:6], refs[6:]
    forward, activated, upper, grads, field, cots, sides = refs
    member, core = place[0], place[1]

    for s in range(4):
        group = (member + s) & 3
        mine, near, far = parts[(0, 3, 3, 3)[s] :][:3]
        base = (0, 52, 0, 26)[s]
        near_row = pl.multiple_of((1 - core) * 128 + group * 16, 16)
        far_row = pl.multiple_of(core * 128 + group * 16, 16)
        own_row = pl.multiple_of(64 + group * 16, 16)
        for row in range(14):
            here = slice(row * LANES, (row + 1) * LANES)
            field[pl.ds(near_row, 16), here] = near[base + row]
            field[pl.ds(own_row, 16), here] = mine[base + row]
            field[pl.ds(far_row, 16), here] = far[base + row]
        cot_row = pl.multiple_of(group * 16, 16)
        near_cot = pl.multiple_of(64 + (1 - core) * 32 + group * 8, 8)
        far_cot = pl.multiple_of(64 + core * 32 + group * 8, 8)
        for row in range(12):
            here = slice(row * LANES, (row + 1) * LANES)
            cots[pl.ds(cot_row, 16), here] = mine[base + 14 + row].astype(F32)
            wide_near = near[base + 14 + row].astype(F32)
            wide_far = far[base + 14 + row].astype(F32)
            cots[pl.ds(near_cot, 8), here] = jnp.where(core == 0, wide_near[0:8], wide_near[8:16])
            cots[pl.ds(far_cot, 8), here] = jnp.where(core == 0, wide_far[8:16], wide_far[0:8])

    upper[:, 0 : 2 * LANES] = jnp.zeros((128, 2 * LANES), BF16)
    upper[:, 14 * LANES : 16 * LANES] = jnp.zeros((128, 2 * LANES), BF16)
    for pair in range(6):
        low = pair * 2
        total = sum(dot(forward[b], field[:, (low + b) * LANES : (low + b + 2) * LANES]) for b in range(3))
        for side in range(2):
            row = low + side
            here = slice(row * LANES, (row + 1) * LANES)
            cut = total[:, side * LANES : (side + 1) * LANES]
            pre = cut[128:256] + shifted(cut[0:128], 1) + shifted(cut[256:384], -1)
            power = jnp.exp(jnp.minimum(pre, 0.0))
            activated[:, here] = jnp.where(pre[:64] > 0, pre[:64], power[:64] - 1.0).astype(BF16)
            cot = cots[:, here]
            up = jnp.where(pre > 0, cot, cot * power).astype(BF16)
            upper[:, (row + 2) * LANES : (row + 3) * LANES] = up
            wide_up = up[:64].astype(F32)
            sides[0:64, here] = shifted(wide_up, -1).astype(BF16)
            sides[64:128, here] = up[:64]
            sides[128:192, here] = shifted(wide_up, 1).astype(BF16)

    row = iota((192, 256), 0)
    col = iota((192, 256), 1)
    row_plane = row // 64 * 2 + row // 8 % 2
    same = row // 16 % 4 * 8 + row % 8 == col % 32
    row9 = iota((192, 128), 0)
    col9 = iota((192, 128), 1)
    plane9 = row9 // 64 * 2 + row9 // 8 % 2
    same9 = row9 // 16 % 4 * 8 + row9 % 8 == col9 % 32
    eight = jnp.zeros((96, 256), F32)
    ninth = jnp.zeros((32, 128), F32)
    for b in range(3):
        product = lax.dot_general(
            sides[...],
            field[:, b * LANES : (12 + b) * LANES],
            (((1,), (1,)), ((), ())),
            preferred_element_type=F32,
        ).reshape(12, 2, 8, 192)
        for x in range(2):
            part = split(product[:, x].reshape(96, 192))
            pick = same & (col // 32 % 3 == b) & (row_plane == 1 + x + col // 96)
            picked = dot(part, one_hot(pick).astype(BF16))
            eight = eight + (picked[0:96] + picked[96:192] + picked[192:288])
            if b == 2:
                for c in range(3):
                    pick = same9 & (col9 // 32 == c) & (plane9 == 3 + x)
                    rows = [part[k * 96 + c * 32 : k * 96 + c * 32 + 32] for k in range(3)]
                    picked = dot(jnp.concatenate(rows, axis=0), one_hot(pick).astype(BF16))
                    ninth = ninth + (picked[0:32] + picked[32:64] + picked[64:96])
    for c in range(3):
        for half in range(2):
            cut = eight[c * 32 : c * 32 + 32, half * LANES : (half + 1) * LANES]
            grads[(c * 2 + half) * 4 : (c * 2 + half) * 4 + 4] = cut.reshape(4, 8, LANES)
    grads[24:28] = ninth.reshape(4, 8, LANES)
    grads[28:32] = jnp.zeros((4, 8, LANES), F32)


def backward_kernel(place, activated, upper, backward, *refs):
    backs, results = refs[:4], refs[4]
    member = place[0]
    for pair in range(7):
        low = pair * 2
        total = sum(dot(backward[b], upper[:, (low + b) * LANES : (low + b + 2) * LANES]) for b in range(3))
        for side in range(2):
            cut = total[:, side * LANES : (side + 1) * LANES]
            grad = cut[64:128] + shifted(cut[0:64], 1) + shifted(cut[128:192], -1)
            results[:, (low + side) * LANES : (low + side + 1) * LANES] = grad.astype(BF16)

    for step, back in enumerate(backs):
        low = pl.multiple_of(((member + step) & 3) * 16, 16)
        for row in range(12):
            back[row] = activated[pl.ds(low, 16), row * LANES : (row + 1) * LANES]
        for row in range(14):
            back[12 + row] = results[pl.ds(low, 16), row * LANES : (row + 1) * LANES]


def call(kernel, outs, scratch=(), place=False, flops=0, moved=0):
    vmem = pl.BlockSpec(memory_space=pltpu.VMEM)
    smem = pl.BlockSpec(memory_space=pltpu.SMEM)

    def run(*args):
        specs = [vmem] * len(args)
        if place:
            specs[0] = smem
        return pl.pallas_call(
            kernel,
            out_shape=outs,
            in_specs=specs,
            out_specs=jax.tree.map(lambda _: vmem, outs),
            scratch_shapes=scratch,
            compiler_params=pltpu.CompilerParams(vmem_limit_bytes=48 * 1024 * 1024),
            cost_estimate=pl.CostEstimate(flops=flops, bytes_accessed=moved, transcendentals=0),
        )(*args)

    return run


def reshard(parts):
    got = [parts[0], None, None, None]
    for step in (1, 3, 2):
        got[4 - step] = lax.ppermute(parts[step], "chan", [(i, (i + step) % 4) for i in range(4)])
    return got


def body(crops, cotangent, weights):
    place = jnp.stack([lax.axis_index("chan"), lax.axis_index("core")]).astype(jnp.int32)
    piece = jax.ShapeDtypeStruct((26, 16, LANES), BF16)
    packed = call(pack_kernel, (piece,) * 4, place=True, flops=10**9)(place, crops[0], cotangent[0])
    got = reshard(packed)
    chips = lax.axis_size("zlo") * lax.axis_size("y")
    remote = [(2 * i + 1, 2 * i + 2) for i in range(chips - 1)]
    remote += [(j, i) for i, j in remote]
    parts = []
    for mine in (got[0], None):
        if mine is None:
            *parts, a, b, c = lax.optimization_barrier((*parts, got[2], got[3], got[1]))
            mine = jnp.concatenate([a, b, c], axis=0)
        near = lax.ppermute(mine, "core", [(0, 1), (1, 0)])
        far = lax.ppermute(mine, ("zlo", "y", "core"), remote)
        parts += [mine, near, far]
    by_out = jnp.transpose(weights, (1, 0, 2)).reshape(864, 32)
    by_in = jnp.transpose(weights, (1, 2, 0)).reshape(864, 32)
    forward, backward = call(
        band_kernel,
        (jax.ShapeDtypeStruct((3, 384, 192), BF16), jax.ShapeDtypeStruct((3, 192, 128), BF16)),
        flops=10**9,
    )(by_out, by_in)
    rows = jax.ShapeDtypeStruct((64, 12 * LANES), BF16)
    activated, upper, grads = call(
        forward_kernel,
        (rows, jax.ShapeDtypeStruct((128, 16 * LANES), BF16), jax.ShapeDtypeStruct((32, 8, LANES), F32)),
        [
            pltpu.VMEM((192, 14 * LANES), BF16),
            pltpu.VMEM((128, 12 * LANES), F32),
            pltpu.VMEM((192, 12 * LANES), BF16),
        ],
        place=True,
        flops=3 * 10**9,
    )(place, *parts, forward)
    piece = jax.ShapeDtypeStruct((26, 16, LANES), BF16)
    backs = call(
        backward_kernel,
        (piece,) * 4,
        [pltpu.VMEM((64, 14 * LANES), BF16)],
        place=True,
        flops=2 * 10**9,
    )(place, activated, upper, backward)
    plane = ("y", "core", "batch")
    column = ("zlo", "chan")
    pieces, rest = lax.axis_size(plane), lax.axis_size(column)
    terms = lax.all_to_all(grads.reshape((pieces, -1) + grads.shape[1:]), plane, 0, 0)
    terms, backs = lax.optimization_barrier((terms, backs))
    share = jnp.sum(terms, axis=0)
    terms = lax.all_to_all(jnp.broadcast_to(share, (rest,) + share.shape), column, 0, 0)
    cells = pieces * rest // lax.axis_size("chan") * crops.shape[2] * crops.shape[3] * crops.shape[4]
    share = jnp.sum(terms, axis=0) / jnp.sqrt(jnp.float32(cells))
    whole = lax.all_to_all(jnp.broadcast_to(share, (pieces,) + share.shape), plane, 0, 0).reshape(32, 8, LANES)
    slab = jax.ShapeDtypeStruct((8, 2, 48, LANES), BF16)
    moves = call(
        moves_kernel,
        (jax.ShapeDtypeStruct((768, 768), BF16), jax.ShapeDtypeStruct((768, 896), BF16)),
        place=True,
        flops=10**9,
    )(place)
    got = reshard(backs)
    activated, input_grad = call(unpack_kernel, (slab, slab), flops=10**9)(*moves, got[0], got[2], got[1], got[3])
    eight = whole[:24].reshape(3, 2, 4, 8, 4, 32).transpose(2, 3, 1, 4, 0, 5).reshape(32, 8, 3, 32)
    ninth = whole[24:28].reshape(32, 1, 4, 32)[:, :, :3]
    weight_grad = jnp.concatenate([eight, ninth], axis=1).reshape(32, 27, 32)
    return activated[None], input_grad[None], weight_grad


def solution(mesh):
    space, chan, batch = (mesh.shape[name] for name in ("space", "chan", "batch"))
    cut = mesh.devices.reshape(space // 8, 4, 2, chan, batch)
    fine = Mesh(cut, ("zlo", "y", "core", "chan", "batch"))
    spec = P("batch", "chan", ("zlo", "y", "core"), None, None)
    return jax.shard_map(
        body,
        mesh=fine,
        in_specs=(spec, spec, P()),
        out_specs=(spec, spec, P()),
        check_vma=False,
    )
```
